512 devices in a mesh: wide: 32 (over y, x), narrow: 16 (over z, core).
Axes of the slice: x: 4, y: 8, z: 8, core: 2. Of those that a mesh axis runs over, the one named last changes fastest.
Arguments:
- hamiltonian: float32 [1024, 3, 128, 128], P(('wide', 'narrow')), may hold values from -3.3 to 3.3, as said below
- old_density: float32 [1024, 3, 128, 128], P(('wide', 'narrow')), may hold values from -2 to 2
- neighbours: int32 [1024, 3], P(('wide', 'narrow')), may hold values from 0 to 31, as said below
- live: int32 [1024], P(('wide', 'narrow')), may hold values from 0 to 1, as said below
- potential: float32 [1], replicated, may hold values from -1 to 1
Outputs:
- density: float32 [1024, 3, 128, 128], P(('wide', 'narrow'))
The draws below stay inside these ranges and needn't reach their ends.
Inputs may be any that keep to these rules, and one draw needn't show every extreme that they name: Within each cluster of 32 consecutive blocks, entry 0 is the block's own index in the cluster and entries 1 and 2 are its neighbours on a cycle through all blocks of the cluster: block a is entry 1 of its entry-2 neighbour and entry 2 of its entry-1 neighbour. Along the cycle the 2 blocks of one device stand next to each other in some order; the devices of the narrow axis follow each other in an order drawn from the seed. For each index of the narrow axis, the devices at wide indices i and i + 16 own at most 2 live blocks together; in every draw some device owns 2 live blocks. `hamiltonian`: the block Hamiltonian is symmetric: tile 1 of block c is the transpose of tile 2 of prev(c), and tile 0 is symmetric.
All inputs are finite; a program needn't handle non-finite values. Where the reference program divides by a largest or mean magnitude, that divisor is 1e-20 or more.
Results may differ from the reference program's by a relative error of at most 0.0001.
Values sent between devices are 32-bit elements; how exact they have to be, the bound alone decides.
A program may use at most 64 MiB of HBM per device.

```python
import jax
import jax.numpy as jnp
from jax import lax

BLK = 128
SUB = 3
BLK_DEV = 2
ITERS = 4
NC = 32
NBLK = 1024


coupling = 0.03


def device_order(owner_key):
    owners = NC // BLK_DEV
    half = owners // 2
    shuffled = jax.random.permutation(owner_key, owners).astype(jnp.int32)
    slots = jnp.arange(owners, dtype=jnp.int32)
    first_pos = jnp.sum(jnp.where(shuffled == 0, slots, 0)).astype(jnp.int32)
    half_pos = jnp.sum(jnp.where(shuffled == half, slots, 0)).astype(jnp.int32)
    after_pos = ((first_pos + 1) % owners).astype(jnp.int32)
    after_value = shuffled[after_pos]
    swapped = jnp.where(slots == after_pos, half, shuffled)
    swapped = jnp.where((slots == half_pos) & (half_pos != after_pos), after_value, swapped)
    return swapped.astype(jnp.int32)


def cycle_lists(key):
    clusters = NBLK // NC
    owners = NC // BLK_DEV
    order_keys = jax.random.split(jax.random.fold_in(key, 11), clusters * owners)

    def owner_order(owner_key):
        return jax.random.permutation(owner_key, BLK_DEV)
    within = jax.vmap(owner_order)(order_keys).astype(jnp.int32).reshape((clusters, owners, BLK_DEV))
    seq_keys = jax.random.split(jax.random.fold_in(key, 17), clusters)
    sequence = jax.vmap(device_order)(seq_keys).astype(jnp.int32)
    orders = (sequence[:, :, None] * BLK_DEV + within).reshape((clusters, NC)).astype(jnp.int32)
    flip = jax.random.randint(jax.random.fold_in(key, 13), (clusters, 1), 0, 2)
    orders = jnp.where(flip == 1, orders[:, ::-1], orders).astype(jnp.int32)
    position = jnp.argsort(orders, axis=1, stable=True).astype(jnp.int32)
    before = jnp.take_along_axis(orders, (position - 1) % NC, axis=1)
    behind = jnp.take_along_axis(orders, (position + 1) % NC, axis=1)
    itself = jnp.broadcast_to(jnp.arange(NC, dtype=jnp.int32)[None, :], position.shape)
    return jnp.stack([itself, before, behind], axis=-1).reshape((NBLK, 3)).astype(jnp.int32)


def draw_neighbours(key, part):
    return cycle_lists(key)


def draw_hamiltonian(key, part):
    local_ids = cycle_lists(key)
    cluster_start = jnp.arange(NBLK, dtype=jnp.int32) // NC * NC
    global_ids = local_ids + cluster_start[:, None]
    tile_key = jax.random.fold_in(key, 23)
    energy_key = jax.random.fold_in(key, 29)
    shape = (NBLK, SUB, BLK, BLK)
    random_tiles = jax.random.truncated_normal(tile_key, -4.0, 4.0, shape, jnp.float32) * coupling
    energies = jax.random.uniform(energy_key, (NBLK, BLK), jnp.float32, -2.5, 2.5)
    mirror_slot = jnp.array([0, 2, 1], dtype=jnp.int32)
    mirrored = random_tiles[global_ids, mirror_slot[None, :]]
    tiles = random_tiles + jnp.swapaxes(mirrored, -1, -2)
    onsite_add = energies[:, :, None] * jnp.eye(BLK, dtype=jnp.float32)[None, :, :]
    tiles = tiles.at[:, 0].add(onsite_add)
    return tiles.astype(jnp.float32)


def draw_live(key, part):
    narrow_count = NC // BLK_DEV
    wide_count = NBLK // NC
    half_count = wide_count // 2
    pair_kind = jax.random.randint(jax.random.fold_in(key, 31), (half_count * narrow_count,), 0, 6)
    forced_pair = jax.random.randint(jax.random.fold_in(key, 37), (), 0, half_count * narrow_count)
    forced_kind = jax.random.randint(jax.random.fold_in(key, 41), (), 0, 2)
    pair_kind = jnp.where(jnp.arange(half_count * narrow_count) == forced_pair, forced_kind, pair_kind)
    pair_kind = pair_kind.reshape((half_count, narrow_count))
    lower_table = jnp.array([2, 0, 1, 1, 0, 0], dtype=jnp.int32)
    upper_table = jnp.array([0, 2, 1, 0, 1, 0], dtype=jnp.int32)
    counts = jnp.concatenate([lower_table[pair_kind], upper_table[pair_kind]], axis=0)
    chosen_slot = jax.random.randint(jax.random.fold_in(key, 43), (wide_count, narrow_count), 0, 2)
    first_live = (counts == 2) | (counts == 1) & (chosen_slot == 0)
    second_live = (counts == 2) | (counts == 1) & (chosen_slot == 1)
    return jnp.stack([first_live, second_live], axis=-1).reshape((NBLK,)).astype(jnp.int32)


def steps_of(rng, shape, pieces, low, high):
    loudness = 1.0
    for dim, blocks in pieces:
        heights = jax.random.uniform(jax.random.fold_in(jax.random.fold_in(rng, 6), dim), (blocks,), jnp.float32, low / len(pieces), high / len(pieces))
        loudness = loudness * jnp.repeat(jnp.exp(heights), shape[dim] // blocks).reshape((-1,) + (1,) * (len(shape) - 1 - dim))
    return loudness


def scatter_about(own_key, dims, deviation, most, shards=(), held_as=jnp.bfloat16):
    entries = deviation * jax.random.normal(own_key, dims, jnp.float32)
    if shards:
        entries = entries * steps_of(own_key, dims, shards, -0.22, 0.18)
    return jnp.clip(entries, -most, most).astype(held_as)


def setup_inputs(seed: int = 0) -> dict:
    key_list = jax.random.split(jax.random.key(seed), 6)
    hamiltonian = draw_hamiltonian(jax.random.fold_in(key_list[5], 71), 0)
    old_density = scatter_about(key_list[1], (NBLK, SUB, BLK, BLK), 0.3, 2.0, ((0, 512),), jnp.float32)
    neighbours = draw_neighbours(jax.random.fold_in(key_list[5], 71), 0)
    live = draw_live(jax.random.fold_in(key_list[5], 71), 0)
    potential = jnp.clip(jax.random.uniform(key_list[4], (1,), jnp.float32, -1.0, 1.0), -1.0, 1.0)
    return dict(hamiltonian=hamiltonian, old_density=old_density, neighbours=neighbours, live=live, potential=potential)


epsilon = 1e-6


def product(left, right):
    return jnp.matmul(left, right, precision=lax.Precision.HIGHEST)


def transpose_tiles(tiles):
    return jnp.swapaxes(tiles, -1, -2)


def assemble(row_tiles, prev_onsite, next_onsite, level):
    zero_tile = jnp.zeros_like(prev_onsite)
    upper_rows = jnp.concatenate([row_tiles[..., 0, :, :], row_tiles[..., 1, :, :], row_tiles[..., 2, :, :]], axis=-1)
    middle_rows = jnp.concatenate([transpose_tiles(row_tiles[..., 1, :, :]), prev_onsite, zero_tile], axis=-1)
    lower_rows = jnp.concatenate([transpose_tiles(row_tiles[..., 2, :, :]), zero_tile, next_onsite], axis=-1)
    matrix = jnp.concatenate([upper_rows, middle_rows, lower_rows], axis=-2)
    order = matrix.shape[-1]
    return matrix - level * jnp.eye(order, dtype=matrix.dtype)


def sign_columns(matrix):
    order = matrix.shape[-1]
    width = order // SUB
    identity = jnp.eye(order, dtype=matrix.dtype)
    bound = jnp.max(jnp.sum(jnp.abs(matrix), axis=-1), axis=-1) + epsilon
    current = matrix / bound
    for sweep in range(ITERS):
        square = product(current, current)
        current = 0.5 * product(current, 3.0 * identity - square)
    columns = 0.5 * (identity[:, :width] - current[:, :width])
    return columns.reshape((SUB, width, width))


def reference(hamiltonian, old_density, neighbours, live, potential):
    level = potential[0]
    cluster_start = (jnp.arange(NBLK, dtype=jnp.int32) // NC * NC).astype(jnp.int32)
    global_ids = (neighbours + cluster_start[:, None]).astype(jnp.int32)
    onsite = hamiltonian[:, 0]

    def solve_block(block_index):
        row_tiles = hamiltonian[block_index]
        prev_onsite = onsite[global_ids[block_index, 1]]
        next_onsite = onsite[global_ids[block_index, 2]]
        return sign_columns(assemble(row_tiles, prev_onsite, next_onsite, level))

    computed = lax.map(solve_block, jnp.arange(NBLK, dtype=jnp.int32))
    fresh_cols = jnp.where(live[:, None, None, None] == 1, computed, old_density)
    from_prev = fresh_cols[global_ids[:, 1], 2]
    from_next = fresh_cols[global_ids[:, 2], 1]
    return jnp.stack([
        0.5 * (fresh_cols[:, 0] + transpose_tiles(fresh_cols[:, 0])),
        0.5 * (fresh_cols[:, 1] + transpose_tiles(from_prev)),
        0.5 * (fresh_cols[:, 2] + transpose_tiles(from_next)),
    ], axis=1)
```

```python
import functools

import jax
import jax.numpy as jnp
from jax import lax
from jax.experimental import pallas as pl
from jax.experimental.pallas import tpu as pltpu
from jax.sharding import PartitionSpec as P

ITERS = 4
EPSILON = 1e-06
BLK = 128
ORDER = 3 * BLK
PEERS = 16
STRIP = BLK // PEERS
F32 = jnp.float32
BF16 = jnp.bfloat16
ALL, FIRST, REST = slice(0, ORDER), slice(0, BLK), slice(BLK, ORDER)


def halves(x):
    high = x.astype(BF16)
    return high, (x - high.astype(F32)).astype(BF16)


def product(left, right):
    lh, ll = left
    rh, rl = right
    return jnp.dot(
        jnp.concatenate([lh, ll, lh], axis=1),
        jnp.concatenate([rh, rh, rl], axis=0),
        preferred_element_type=F32,
    )


def kernel(
    ham, old, nbr, live, pot, out,
    packed, note, got_strip, got_note, pick, whole,
    x_all, xh_all, xl_all, sh_all, sl_all,
    edge, got_edge, pick_edge, whole_edge, rows_out,
    send, recv,
):
    w = lax.axis_index("wide")
    n = lax.axis_index("narrow")

    def peer(j):
        return (w, (n + j) & (PEERS - 1))

    barrier = pltpu.get_barrier_semaphore()

    def greet(j, _):
        pl.semaphore_signal(barrier, inc=1, device_id=peer(j), device_id_type=pl.DeviceIdType.MESH)
        return _

    lax.fori_loop(1, PEERS, greet, 0)

    forward = nbr[0, 2] == 2 * n + 1
    a = jnp.where(forward, 0, 1)
    b = 1 - a
    prev_off = ((nbr[a, 1] >> 1) - n) & (PEERS - 1)
    next_off = ((nbr[b, 2] >> 1) - n) & (PEERS - 1)

    row = lax.broadcasted_iota(jnp.int32, (BLK, BLK), 0)
    col = lax.broadcasted_iota(jnp.int32, (BLK, BLK), 1)
    diagonal = row == col
    on_a = ham[a, 0]
    on_b = ham[b, 0]
    packed[...] = jnp.where(col >= row, on_a, on_b).reshape(PEERS, STRIP, BLK)
    note[0, :, 0:BLK] = jnp.sum(jnp.where(diagonal, on_b, 0.0), axis=0, keepdims=True)
    note[0, :, BLK : 2 * BLK] = jnp.full((1, BLK), prev_off, jnp.int32).astype(F32)
    note[0, :, 2 * BLK : 3 * BLK] = jnp.full((1, BLK), next_off, jnp.int32).astype(F32)

    def push(src, dst, which, j):
        return pltpu.make_async_remote_copy(
            src_ref=src, dst_ref=dst, send_sem=send.at[which], recv_sem=recv.at[which],
            device_id=peer(j), device_id_type=pl.DeviceIdType.MESH,
        )

    def wait_all(ref, sem):
        many = ref.at[pl.ds(1, PEERS - 1)]
        pltpu.make_async_copy(many, many, sem).wait()

    pl.semaphore_wait(barrier, PEERS - 1)

    def first(j, _):
        push(note.at[0], got_note.at[j], 1, j).start()
        push(packed.at[(n + j) & (PEERS - 1)], got_strip.at[j], 0, j).start()
        return _

    lax.fori_loop(1, PEERS, first, 0)
    got_strip[0] = packed[n]
    got_note[0] = note[0]
    wait_all(got_note, recv.at[1])
    wait_all(got_strip, recv.at[0])

    below = (
        lax.broadcasted_iota(jnp.int32, (STRIP, BLK), 1)
        < lax.broadcasted_iota(jnp.int32, (STRIP, BLK), 0) + STRIP * n
    )

    def offsets(j):
        slot = (PEERS - j) & (PEERS - 1)
        return got_note[slot, :, BLK : 2 * BLK], got_note[slot, :, 2 * BLK : 3 * BLK]

    def route(j):
        to_prev, to_next = offsets(j)
        wanted = jnp.where(below, to_prev, to_next)
        chosen = jnp.zeros((STRIP, BLK), F32)
        for k in range(PEERS):
            offset = ((-j - k) & (PEERS - 1))
            chosen = jnp.where(wanted == offset, got_strip[k], chosen)
        return chosen

    for j in range(1, PEERS):
        pick[j] = route(j)
        push(pick.at[j], whole.at[n], 2, j).start()
    whole[n] = route(0)

    to_prev, to_next = offsets(0)
    far_diag = jnp.zeros((1, BLK), F32)
    for k in range(PEERS):
        far_diag = jnp.where(to_prev == ((-k) & (PEERS - 1)), got_note[k, :, 0:BLK], far_diag)

    wait_all(whole, recv.at[2])
    upper = whole[...].reshape(BLK, BLK)
    mirror = upper.T
    on_next = jnp.where(col >= row, upper, mirror)
    on_prev = jnp.where(col < row, upper, mirror)
    on_prev = jnp.where(diagonal, far_diag, on_prev)

    level = jnp.where(diagonal, pot[0], 0.0)

    def block(s):
        return x_all.at[s], xh_all.at[s], xl_all.at[s], sh_all.at[s], sl_all.at[s]

    def put(high, low, rows, cols, value):
        high[rows, cols], low[rows, cols] = halves(value)

    def assemble(s, here, before, behind):
        x, xh, xl, sh, sl = block(s)
        index = a if s == 0 else b
        t1, t2 = ham[index, 1], ham[index, 2]
        t1t = t1.T
        t2t = t2.T
        d0, d1, d2 = here - level, before - level, behind - level

        def sums(*tiles):
            return functools.reduce(jnp.add, [jnp.sum(jnp.abs(t), axis=0, keepdims=True) for t in tiles])

        most = jnp.maximum(jnp.maximum(sums(d0, t1t, t2t), sums(t1, d1)), sums(t2, d2))
        scale = 1.0 / (jnp.max(most, axis=1, keepdims=True) + EPSILON)
        tiles = ((d0, t1, t2), (t1t, d1, None), (t2t, None, d2))
        for i in range(3):
            for k in range(3):
                rows, cols = slice(BLK * i, BLK * i + BLK), slice(BLK * k, BLK * k + BLK)
                if tiles[i][k] is None:
                    value = jnp.zeros((BLK, BLK), F32)
                else:
                    value = tiles[i][k] * scale
                x[rows, cols] = value
                put(xh, xl, rows, cols, value)

    def mirrored(high, low, rest):
        put(high, low, slice(BLK, 2 * BLK), FIRST, rest[0:BLK, 0:BLK].T)
        put(high, low, slice(2 * BLK, 3 * BLK), FIRST, rest[0:BLK, BLK : 2 * BLK].T)

    def square(s):
        x, xh, xl, sh, sl = block(s)
        rest = product((xh[...], xl[...]), (xh[:, REST], xl[:, REST]))
        put(sh, sl, ALL, REST, rest)
        corner = product((xh[FIRST, :], xl[FIRST, :]), (xh[:, FIRST], xl[:, FIRST]))
        put(sh, sl, FIRST, FIRST, corner)
        mirrored(sh, sl, rest)

    def advance(s):
        x, xh, xl, sh, sl = block(s)
        rest = 1.5 * x[:, REST] - 0.5 * product((xh[...], xl[...]), (sh[:, REST], sl[:, REST]))
        x[:, REST] = rest
        corner = 1.5 * x[FIRST, FIRST] - 0.5 * product(
            (xh[FIRST, :], xl[FIRST, :]), (sh[:, FIRST], sl[:, FIRST])
        )
        x[FIRST, FIRST] = corner
        put(xh, xl, ALL, REST, rest)
        put(xh, xl, FIRST, FIRST, corner)
        mirrored(xh, xl, rest)

    def finish(s):
        x, xh, xl, sh, sl = block(s)
        whole_x = (xh[...], xl[...])
        thin = product((xh[FIRST, :], xl[FIRST, :]), whole_x)
        rows_out[s] = 1.5 * x[FIRST, :] - 0.5 * product(halves(thin), whole_x)

    assemble(0, on_a, on_prev, on_b)
    assemble(1, on_b, on_a, on_next)
    for sweep in range(ITERS - 1):
        square(0)
        square(1)
        advance(0)
        advance(1)
    finish(0)
    finish(1)

    unit = jnp.where(diagonal, 1.0, 0.0)

    def fresh(s, j):
        index = a if s == 0 else b
        x = rows_out[s, :, BLK * j : BLK * j + BLK]
        new = 0.5 * (unit - x) if j == 0 else -0.5 * x
        return jnp.where(live[index] == 1, new, old[index, j].T)

    f1a, f2b = fresh(0, 1), fresh(1, 2)
    edge[:, 0:STRIP, :] = f1a.reshape(PEERS, STRIP, BLK)
    edge[:, STRIP : 2 * STRIP, :] = f2b.reshape(PEERS, STRIP, BLK)

    def second(j, _):
        push(edge.at[(n + j) & (PEERS - 1)], got_edge.at[j], 3, j).start()
        return _

    lax.fori_loop(1, PEERS, second, 0)
    got_edge[0] = edge[n]
    wait_all(got_edge, recv.at[3])

    def route_edge(j):
        to_prev, to_next = offsets(j)
        to_prev = jnp.broadcast_to(to_prev, (STRIP, BLK))
        to_next = jnp.broadcast_to(to_next, (STRIP, BLK))
        from_prev = jnp.zeros((STRIP, BLK), F32)
        from_next = jnp.zeros((STRIP, BLK), F32)
        for k in range(PEERS):
            offset = ((-j - k) & (PEERS - 1))
            from_prev = jnp.where(to_prev == offset, got_edge[k, STRIP : 2 * STRIP], from_prev)
            from_next = jnp.where(to_next == offset, got_edge[k, 0:STRIP], from_next)
        return from_prev, from_next

    for j in range(1, PEERS):
        pick_edge[j, 0:STRIP], pick_edge[j, STRIP : 2 * STRIP] = route_edge(j)
        push(pick_edge.at[j], whole_edge.at[n], 4, j).start()
    whole_edge[n, 0:STRIP], whole_edge[n, STRIP : 2 * STRIP] = route_edge(0)

    f0a, f2a, f0b, f1b = fresh(0, 0), fresh(0, 2), fresh(1, 0), fresh(1, 1)

    def emit(j, of_a, of_b):
        out[0, j] = jnp.where(forward, of_a, of_b)
        out[1, j] = jnp.where(forward, of_b, of_a)

    emit(0, 0.5 * (f0a + f0a.T), 0.5 * (f0b + f0b.T))
    inner = 0.5 * (f2a.T + f1b)
    f1at, f2bt, innert = f1a.T, f2b.T, inner.T

    wait_all(whole_edge, recv.at[4])
    outer_a = 0.5 * (f1at + whole_edge[:, 0:STRIP, :].reshape(BLK, BLK))
    outer_b = 0.5 * (f2bt + whole_edge[:, STRIP : 2 * STRIP, :].reshape(BLK, BLK))
    emit(1, outer_a, innert)
    emit(2, inner, outer_b)

    wait_all(got_strip, send.at[0])
    wait_all(got_note, send.at[1])
    wait_all(pick, send.at[2])
    wait_all(got_edge, send.at[3])
    wait_all(pick_edge, send.at[4])


def shards(hamiltonian, old_density, neighbours, live, potential):
    vmem = pl.BlockSpec(memory_space=pltpu.VMEM)
    smem = pl.BlockSpec(memory_space=pltpu.SMEM)
    return pl.pallas_call(
        kernel,
        out_shape=jax.ShapeDtypeStruct((2, 3, BLK, BLK), F32),
        in_specs=[vmem, vmem, smem, smem, smem],
        out_specs=vmem,
        scratch_shapes=[
            pltpu.VMEM((PEERS, STRIP, BLK), F32),
            pltpu.VMEM((1, 1, 3 * BLK), F32),
            pltpu.VMEM((PEERS, STRIP, BLK), F32),
            pltpu.VMEM((PEERS, 1, 3 * BLK), F32),
            pltpu.VMEM((PEERS, STRIP, BLK), F32),
            pltpu.VMEM((PEERS, STRIP, BLK), F32),
            pltpu.VMEM((2, ORDER, ORDER), F32),
            pltpu.VMEM((2, ORDER, ORDER), BF16),
            pltpu.VMEM((2, ORDER, ORDER), BF16),
            pltpu.VMEM((2, ORDER, ORDER), BF16),
            pltpu.VMEM((2, ORDER, ORDER), BF16),
            pltpu.VMEM((PEERS, 2 * STRIP, BLK), F32),
            pltpu.VMEM((PEERS, 2 * STRIP, BLK), F32),
            pltpu.VMEM((PEERS, 2 * STRIP, BLK), F32),
            pltpu.VMEM((PEERS, 2 * STRIP, BLK), F32),
            pltpu.VMEM((2, BLK, ORDER), F32),
            pltpu.SemaphoreType.DMA((5,)),
            pltpu.SemaphoreType.DMA((5,)),
        ],
        compiler_params=pltpu.CompilerParams(
            collective_id=0, has_side_effects=True, vmem_limit_bytes=48 * 2**20
        ),
        name="density",
    )(hamiltonian, old_density, neighbours, live, potential)


def solution(mesh):
    placed = (
        P(("wide", "narrow"), None, None, None),
        P(("wide", "narrow"), None, None, None),
        P(("wide", "narrow"), None),
        P(("wide", "narrow")),
        P(),
    )
    return jax.shard_map(
        shards,
        mesh=mesh,
        in_specs=placed,
        out_specs=P(("wide", "narrow"), None, None, None),
        check_vma=False,
    )
```

```python
import functools

import jax
import jax.numpy as jnp
from jax import lax
from jax.experimental import pallas as pl
from jax.experimental.pallas import tpu as pltpu
from jax.sharding import PartitionSpec as P

ITERS = 4
EPSILON = 1e-06
BLK = 128
ORDER = 3 * BLK
PEERS = 16
STRIP = BLK // PEERS
F32 = jnp.float32
BF16 = jnp.bfloat16
ALL, FIRST = slice(0, ORDER), slice(0, BLK)


def halves(x):
    high = x.astype(BF16)
    return high, (x - high.astype(F32)).astype(BF16)


def product(left, right):
    lh, ll = left
    rh, rl = right
    return jnp.dot(
        jnp.concatenate([lh, ll, lh], axis=1),
        jnp.concatenate([rh, rh, rl], axis=0),
        preferred_element_type=F32,
    )


def kernel(
    ham_hbm, old_hbm, nbr_hbm, live_hbm, pot_hbm, out,
    ham, old, nbr, live, pot,
    packed, outer, note, got_packed, got_outer, got_note,
    pick_near, pick_far, near, far, turned,
    x_all, xh_all, xl_all, sh_all, sl_all,
    load, send, recv,
):
    w = lax.axis_index("wide")
    n = lax.axis_index("narrow")

    def peer(j):
        return (w, (n + j) & (PEERS - 1))

    inputs = ((nbr_hbm, nbr), (ham_hbm, ham), (live_hbm, live), (old_hbm, old), (pot_hbm, pot))
    loads = [pltpu.make_async_copy(src, dst, load.at[i]) for i, (src, dst) in enumerate(inputs)]
    for copy in loads:
        copy.start()

    barrier = pltpu.get_barrier_semaphore()

    def greet(j, _):
        pl.semaphore_signal(barrier, inc=1, device_id=peer(j), device_id_type=pl.DeviceIdType.MESH)
        return _

    lax.fori_loop(1, PEERS, greet, 0)

    for copy in loads:
        copy.wait()

    forward = nbr[0, 2] == 2 * n + 1
    a = jnp.where(forward, 0, 1)
    b = 1 - a
    live_a, live_b = live[a], live[b]

    row = lax.broadcasted_iota(jnp.int32, (BLK, BLK), 0)
    col = lax.broadcasted_iota(jnp.int32, (BLK, BLK), 1)
    diagonal = row == col
    on_a = ham[a, 0]
    on_b = ham[b, 0]
    packed[...] = jnp.where(col >= row, on_a, on_b).reshape(PEERS, STRIP, BLK)
    outer[:, 0:STRIP] = jnp.where(live_a == 1, ham[a, 2], old[a, 1]).reshape(PEERS, STRIP, BLK)
    outer[:, STRIP : 2 * STRIP] = jnp.where(live_b == 1, ham[b, 1], old[b, 2]).reshape(PEERS, STRIP, BLK)
    note[0, :, 0:BLK] = jnp.sum(jnp.where(diagonal, on_b, 0.0), axis=0, keepdims=True)
    facts = (
        ((nbr[a, 1] >> 1) - n) & (PEERS - 1), ((nbr[b, 2] >> 1) - n) & (PEERS - 1), live_a, live_b,
    )
    for i, fact in enumerate(facts):
        note[0, :, BLK * (i + 1) : BLK * (i + 2)] = jnp.full((1, BLK), fact, jnp.int32).astype(F32)

    def push(src, dst, which, j):
        return pltpu.make_async_remote_copy(
            src_ref=src, dst_ref=dst, send_sem=send.at[which], recv_sem=recv.at[which],
            device_id=peer(j), device_id_type=pl.DeviceIdType.MESH,
        )

    def wait_all(ref, sem):
        many = ref.at[pl.ds(1, PEERS - 1)]
        pltpu.make_async_copy(many, many, sem).wait()

    pl.semaphore_wait(barrier, PEERS - 1)

    def first(j, _):
        push(note.at[0], got_note.at[j], 0, j).start()
        push(packed.at[(n + j) & (PEERS - 1)], got_packed.at[j], 1, j).start()
        return _

    lax.fori_loop(1, PEERS, first, 0)

    def second(j, _):
        push(outer.at[(n + j) & (PEERS - 1)], got_outer.at[j], 2, j).start()
        return _

    lax.fori_loop(1, PEERS, second, 0)
    got_packed[0] = packed[n]
    got_note[0] = note[0]
    got_outer[0] = outer[n]

    level = jnp.where(diagonal, pot[0], 0.0)
    turned[0] = ham[a, 1].T
    turned[1] = ham[b, 2].T

    wait_all(got_note, recv.at[0])
    wait_all(got_packed, recv.at[1])

    below = (
        lax.broadcasted_iota(jnp.int32, (STRIP, BLK), 1)
        < lax.broadcasted_iota(jnp.int32, (STRIP, BLK), 0) + STRIP * n
    )

    def part(slot, i):
        return got_note[slot, :, BLK * i : BLK * (i + 1)]

    def offsets(j):
        slot = (PEERS - j) & (PEERS - 1)
        return (
            jnp.broadcast_to(part(slot, 1), (STRIP, BLK)),
            jnp.broadcast_to(part(slot, 2), (STRIP, BLK)),
        )

    def select(j, wanted, slots):
        chosen = slots(0)
        for k in range(1, PEERS):
            chosen = jnp.where(wanted == ((-j - k) & (PEERS - 1)), slots(k), chosen)
        return chosen

    def route_near(j):
        to_prev, to_next = offsets(j)
        return select(j, jnp.where(below, to_prev, to_next), lambda k: got_packed[k])

    for j in range(1, PEERS):
        pick_near[j] = route_near(j)
        push(pick_near.at[j], near.at[n], 3, j).start()
    near[n] = route_near(0)

    wait_all(got_outer, recv.at[2])

    def route_far(j, ref):
        to_prev, to_next = offsets(j)
        ref[0:STRIP] = select(j, jnp.where(below, to_next, to_prev), lambda k: got_packed[k])
        ref[STRIP : 2 * STRIP] = select(j, to_prev, lambda k: got_outer[k, STRIP : 2 * STRIP])
        ref[2 * STRIP : 3 * STRIP] = select(j, to_next, lambda k: got_outer[k, 0:STRIP])

    for j in range(1, PEERS):
        route_far(j, pick_far.at[j])
        push(pick_far.at[j], far.at[n], 4, j).start()
    route_far(0, far.at[n])

    def noted(i, which):
        return select(0, part(0, which), lambda k: part(k, i))

    diag_prev, diag_next = noted(0, 1), noted(0, 2)
    live_prev, live_next = noted(4, 1), noted(3, 2)

    def unpack(tile, low_diag):
        mirror = tile.T
        high = jnp.where(col >= row, tile, mirror)
        low = jnp.where(diagonal, low_diag, jnp.where(col < row, tile, mirror))
        return high, low

    wait_all(near, recv.at[3])
    on_next, on_prev = unpack(near[...].reshape(BLK, BLK), diag_prev)

    def block(s):
        return x_all.at[s], xh_all.at[s], xl_all.at[s], sh_all.at[s], sl_all.at[s]

    def tile(i):
        return slice(BLK * i, BLK * i + BLK)

    def put(high, low, rows, cols, value):
        high[rows, cols], low[rows, cols] = halves(value)

    def assemble(s, here, before, behind, t1, t1t, t2, t2t):
        x, xh, xl, sh, sl = block(s)
        d0, d1, d2 = here - level, before - level, behind - level

        def sums(*tiles):
            return functools.reduce(jnp.add, [jnp.sum(jnp.abs(t), axis=0, keepdims=True) for t in tiles])

        most = jnp.maximum(jnp.maximum(sums(d0, t1t, t2t), sums(t1, d1)), sums(t2, d2))
        scale = 1.0 / (jnp.max(most, axis=1, keepdims=True) + EPSILON)
        tiles = ((d0, t1, t2), (t1t, d1, None), (t2t, None, d2))
        for i in range(3):
            for k in range(3):
                rows, cols = tile(i), tile(k)
                if tiles[i][k] is None:
                    value = jnp.zeros((BLK, BLK), F32)
                else:
                    value = tiles[i][k] * scale
                x[rows, cols] = value
                put(xh, xl, rows, cols, value)

    def symmetric(left, right):
        lh, ll = left
        rh, rl = right

        def pair(ref, i):
            return jnp.concatenate([ref[:, tile(i)], ref[:, tile((i + 1) % 3)]], axis=1)

        return [
            product((lh[tile(i), :], ll[tile(i), :]), (pair(rh, i), pair(rl, i))) for i in range(3)
        ]

    def square(s):
        x, xh, xl, sh, sl = block(s)
        for i, both in enumerate(symmetric((xh, xl), (xh, xl))):
            here, after = tile(i), tile((i + 1) % 3)
            put(sh, sl, here, here, both[:, 0:BLK])
            put(sh, sl, here, after, both[:, BLK : 2 * BLK])
            put(sh, sl, after, here, both[:, BLK : 2 * BLK].T)

    def advance(s):
        x, xh, xl, sh, sl = block(s)
        for i, both in enumerate(symmetric((xh, xl), (sh, sl))):
            here, after = tile(i), tile((i + 1) % 3)
            own = 1.5 * x[here, here] - 0.5 * both[:, 0:BLK]
            side = 1.5 * x[here, after] - 0.5 * both[:, BLK : 2 * BLK]
            turn = side.T
            x[here, here] = own
            x[here, after] = side
            if i == 2:
                x[after, here] = turn
            put(xh, xl, here, here, own)
            put(xh, xl, here, after, side)
            put(xh, xl, after, here, turn)

    def finish(s, cols):
        x, xh, xl, sh, sl = block(s)
        thin = product((xh[FIRST, :], xl[FIRST, :]), (xh[...], xl[...]))
        return 1.5 * x[FIRST, cols] - 0.5 * product(halves(thin), (xh[:, cols], xl[:, cols]))

    def iterate(s, t):
        for sweep in range(ITERS - 1):
            square(s)
            square(t)
            advance(s)
            advance(t)

    assemble(0, on_a, on_prev, on_b, ham[a, 1], turned[0], ham[a, 2], ham[b, 1])
    assemble(1, on_b, on_a, on_next, ham[b, 1], ham[a, 2], ham[b, 2], turned[1])
    iterate(0, 1)
    new_a, new_b = finish(0, ALL), finish(1, ALL)

    unit = jnp.where(diagonal, 1.0, 0.0)

    def fresh(new, index, j):
        x = new[:, tile(j)]
        value = 0.5 * (unit - x) if j == 0 else -0.5 * x
        return jnp.where(live[index] == 1, value, old[index, j].T)

    f0a, f1a, f2a = [fresh(new_a, a, j) for j in range(3)]
    f0b, f1b, f2b = [fresh(new_b, b, j) for j in range(3)]

    def emit(j, of_a, of_b):
        out[0, j] = jnp.where(forward, of_a, of_b)
        out[1, j] = jnp.where(forward, of_b, of_a)

    emit(0, 0.5 * (f0a + f0a.T), 0.5 * (f0b + f0b.T))
    inner = 0.5 * (f2a.T + f1b)
    out[0, 1] = f1a.T
    out[1, 1] = inner.T
    out[0, 2] = inner
    out[1, 2] = f2b.T

    wait_all(far, recv.at[4])
    on_prev_prev, on_next_next = unpack(far[:, 0:STRIP].reshape(BLK, BLK), diag_next)
    far_prev = far[:, STRIP : 2 * STRIP].reshape(BLK, BLK)
    far_next = far[:, 2 * STRIP : 3 * STRIP].reshape(BLK, BLK)
    far_prev_t, far_next_t = far_prev.T, far_next.T
    on_next, on_prev = unpack(near[...].reshape(BLK, BLK), diag_prev)
    assemble(2, on_prev, on_prev_prev, on_a, far_prev, far_prev_t, turned[0], ham[a, 1])
    assemble(3, on_next, on_b, on_next_next, turned[1], ham[b, 2], far_next, far_next_t)
    iterate(2, 3)
    edge_prev = jnp.where(live_prev == 1.0, -0.5 * finish(2, tile(2)), far_prev_t)
    edge_next = jnp.where(live_next == 1.0, -0.5 * finish(3, tile(1)), far_next_t)
    outer_a = 0.5 * (out[0, 1] + edge_prev)
    outer_b = 0.5 * (out[1, 2] + edge_next)
    emit(1, outer_a, out[1, 1])
    emit(2, out[0, 2], outer_b)

    wait_all(got_note, send.at[0])
    wait_all(got_packed, send.at[1])
    wait_all(got_outer, send.at[2])
    wait_all(near, send.at[3])
    wait_all(far, send.at[4])


def shards(hamiltonian, old_density, neighbours, live, potential):
    hbm = pl.BlockSpec(memory_space=pltpu.HBM)
    strips = pltpu.VMEM((PEERS, STRIP, BLK), F32)
    two_strips = pltpu.VMEM((PEERS, 2 * STRIP, BLK), F32)
    three_strips = pltpu.VMEM((PEERS, 3 * STRIP, BLK), F32)
    matrices = pltpu.VMEM((4, ORDER, ORDER), F32)
    matrix_halves = pltpu.VMEM((4, ORDER, ORDER), BF16)
    return pl.pallas_call(
        kernel,
        out_shape=jax.ShapeDtypeStruct((2, 3, BLK, BLK), F32),
        in_specs=[hbm] * 5,
        out_specs=pl.BlockSpec(memory_space=pltpu.VMEM),
        scratch_shapes=[
            pltpu.VMEM((2, 3, BLK, BLK), F32),
            pltpu.VMEM((2, 3, BLK, BLK), F32),
            pltpu.SMEM((2, 3), jnp.int32),
            pltpu.SMEM((2,), jnp.int32),
            pltpu.SMEM((1,), F32),
            strips, two_strips, pltpu.VMEM((1, 1, 5 * BLK), F32),
            strips, two_strips, pltpu.VMEM((PEERS, 1, 5 * BLK), F32),
            strips, three_strips, strips, three_strips,
            pltpu.VMEM((2, BLK, BLK), F32),
            matrices, matrix_halves, matrix_halves, matrix_halves, matrix_halves,
            pltpu.SemaphoreType.DMA((5,)),
            pltpu.SemaphoreType.DMA((5,)),
            pltpu.SemaphoreType.DMA((5,)),
        ],
        compiler_params=pltpu.CompilerParams(
            collective_id=0, has_side_effects=True, vmem_limit_bytes=60 * 2**20
        ),
        name="density",
    )(hamiltonian, old_density, neighbours, live, potential)


def solution(mesh):
    placed = (
        P(("wide", "narrow"), None, None, None),
        P(("wide", "narrow"), None, None, None),
        P(("wide", "narrow"), None),
        P(("wide", "narrow")),
        P(),
    )
    return jax.shard_map(
        shards,
        mesh=mesh,
        in_specs=placed,
        out_specs=P(("wide", "narrow"), None, None, None),
        check_vma=False,
    )
```

```python
import functools

import jax
import jax.numpy as jnp
from jax import lax
from jax.experimental import pallas as pl
from jax.experimental.pallas import tpu as pltpu
from jax.sharding import PartitionSpec as P

ITERS = 4
EPSILON = 1e-06
VMEM_LIMIT = 54_580 * 1024
BLK = 128
ORDER = 3 * BLK
PEERS = 16
STRIP = BLK // PEERS
FIELD = BLK // 4
ORDER_OUT = sorted(range(1, PEERS), key=lambda j: abs(j - PEERS // 2))
F32 = jnp.float32
BF16 = jnp.bfloat16
ALL, FIRST = slice(0, ORDER), slice(0, BLK)


def halves(x):
    high = x.astype(BF16)
    return high, (x - high.astype(F32)).astype(BF16)


def product(left, right):
    lh, ll = left
    rh, rl = right
    return jnp.dot(
        jnp.concatenate([lh, ll, lh], axis=1),
        jnp.concatenate([rh, rh, rl], axis=0),
        preferred_element_type=F32,
    )


def kernel(
    ham_hbm, old_hbm, nbr_hbm, live_hbm, pot_hbm, out,
    ham, old, nbr, live, pot,
    packed, outer_next, outer_prev, note, got_packed, got_next, got_prev, got_note,
    pick_near, pick_far, pick_last, near, far, last, turned, base,
    x_all, xh_all, xl_all, sh_all, sl_all,
    load, send, recv,
):
    w = lax.axis_index("wide")
    n = lax.axis_index("narrow")

    def peer(j):
        return (w, (n + j) & (PEERS - 1))

    inputs = ((nbr_hbm, nbr), (ham_hbm, ham), (live_hbm, live), (old_hbm, old), (pot_hbm, pot))
    loads = [pltpu.make_async_copy(src, dst, load.at[i]) for i, (src, dst) in enumerate(inputs)]
    for copy in loads:
        copy.start()

    barrier = pltpu.get_barrier_semaphore()

    def greet(j, _):
        pl.semaphore_signal(barrier, inc=1, device_id=peer(j), device_id_type=pl.DeviceIdType.MESH)
        return _

    lax.fori_loop(1, PEERS, greet, 0)

    for copy in loads:
        copy.wait()

    forward = nbr[0, 2] == 2 * n + 1
    a = jnp.where(forward, 0, 1)
    b = 1 - a
    live_a, live_b = live[a], live[b]

    row = lax.broadcasted_iota(jnp.int32, (BLK, BLK), 0)
    col = lax.broadcasted_iota(jnp.int32, (BLK, BLK), 1)
    diagonal = row == col
    on_a = ham[a, 0]
    on_b = ham[b, 0]
    packed[...] = jnp.where(col >= row, on_a, on_b).reshape(PEERS, STRIP, BLK)
    outer_prev[...] = jnp.where(live_a == 1, ham[a, 2], old[a, 1]).reshape(PEERS, STRIP, BLK)
    outer_next[...] = jnp.where(live_b == 1, ham[b, 1], old[b, 2]).reshape(PEERS, STRIP, BLK)
    note[0, :, 0:BLK] = jnp.sum(jnp.where(diagonal, on_b, 0.0), axis=0, keepdims=True)
    facts = (
        ((nbr[a, 1] >> 1) - n) & (PEERS - 1), ((nbr[b, 2] >> 1) - n) & (PEERS - 1), live_a, live_b,
    )
    lane = lax.broadcasted_iota(jnp.int32, (1, BLK), 1)
    told = jnp.full((1, BLK), facts[0], jnp.int32)
    for i in range(1, 4):
        told = jnp.where(lane >= FIELD * i, facts[i], told)
    note[0, :, BLK : 2 * BLK] = told.astype(F32)

    def push(src, dst, which, j):
        return pltpu.make_async_remote_copy(
            src_ref=src, dst_ref=dst, send_sem=send.at[which], recv_sem=recv.at[which],
            device_id=peer(j), device_id_type=pl.DeviceIdType.MESH,
        )

    def wait_all(ref, sem):
        many = ref.at[pl.ds(1, PEERS - 1)]
        pltpu.make_async_copy(many, many, sem).wait()

    pl.semaphore_wait(barrier, PEERS - 1)

    def to_all(*moves):
        def step(m, _):
            j = PEERS // 2 + (1 - 2 * (m & 1)) * ((m + 1) >> 1)
            for src, dst, which in moves:
                push(src.at[0 if src is note else (n + j) & (PEERS - 1)], dst.at[j], which, j).start()
            return _

        lax.fori_loop(0, PEERS - 1, step, 0)

    to_all((note, got_note, 0), (packed, got_packed, 1))
    to_all((outer_next, got_next, 2))
    to_all((outer_prev, got_prev, 3))
    got_note[0] = note[0]
    got_packed[0] = packed[n]
    got_next[0] = outer_next[n]
    got_prev[0] = outer_prev[n]

    level = jnp.where(diagonal, pot[0], 0.0)

    def block(s):
        return x_all.at[s], xh_all.at[s], xl_all.at[s], sh_all.at[s], sl_all.at[s]

    def tile(i):
        return slice(BLK * i, BLK * i + BLK)

    def put(high, low, rows, cols, value):
        high[rows, cols], low[rows, cols] = halves(value)

    def sums(*tiles):
        return functools.reduce(jnp.add, [jnp.sum(jnp.abs(t), axis=0, keepdims=True) for t in tiles])

    def scale_of(most):
        return 1.0 / (jnp.max(most, axis=1, keepdims=True) + EPSILON)

    def assemble(s, tiles):
        x, xh, xl, sh, sl = block(s)
        for i in range(3):
            for k in range(3):
                rows, cols = tile(i), tile(k)
                value = jnp.zeros((BLK, BLK), F32) if tiles[i][k] is None else tiles[i][k]
                x[rows, cols] = value
                put(xh, xl, rows, cols, value)

    def symmetric(left, right, first):
        def strip(ref, i, inner):
            return jnp.concatenate([ref[tile(i), tile(k)] for k in inner], axis=1)

        def pair(ref, i, inner):
            return jnp.concatenate([
                jnp.concatenate([ref[tile(k), tile(i)], ref[tile(k), tile((i + 1) % 3)]], axis=1)
                for k in inner
            ], axis=0)

        results = []
        for i in range(3):
            inner = (0, i) if first and i > 0 else (0, 1, 2)
            results.append(product(
                tuple(strip(ref, i, inner) for ref in left), tuple(pair(ref, i, inner) for ref in right)
            ))
        return results

    def square(s, first=False, keep=None):
        x, xh, xl, sh, sl = block(s)
        for i, both in enumerate(symmetric((xh, xl), (xh, xl), first)):
            here, after = tile(i), tile((i + 1) % 3)
            own, side = both[:, 0:BLK], both[:, BLK : 2 * BLK]
            put(sh, sl, here, here, own)
            put(sh, sl, here, after, side)
            put(sh, sl, after, here, side.T)
            if keep is not None and i == keep:
                base[s, 0] = own
            if keep is not None and i == 0 and keep == 1:
                base[s, 1] = side.T
            if keep is not None and i == 2 and keep == 2:
                base[s, 1] = side

    def complete(s, u, value):
        x, xh, xl, sh, sl = block(s)
        mine = tile(u)
        x[mine, mine] = value
        vh, vl = halves(value)
        xh[mine, mine], xl[mine, mine] = vh, vl
        more = product(
            (vh, vl),
            (
                jnp.concatenate([xh[mine, FIRST], vh], axis=1),
                jnp.concatenate([xl[mine, FIRST], vl], axis=1),
            ),
        )
        side = base[s, 1] + more[:, 0:BLK]
        put(sh, sl, mine, FIRST, side)
        put(sh, sl, FIRST, mine, side.T)
        put(sh, sl, mine, mine, base[s, 0] + more[:, BLK : 2 * BLK])

    def advance(s, scale=None):
        x, xh, xl, sh, sl = block(s)
        once, thrice = (1.5, 0.5) if scale is None else (1.5 * scale, 0.5 * scale * scale * scale)
        for i, both in enumerate(symmetric((xh, xl), (sh, sl), scale is not None)):
            here, after = tile(i), tile((i + 1) % 3)
            own = once * x[here, here] - thrice * both[:, 0:BLK]
            side = once * x[here, after] - thrice * both[:, BLK : 2 * BLK]
            turn = side.T
            x[here, here] = own
            x[here, after] = side
            if i == 2:
                x[after, here] = turn
            put(xh, xl, here, here, own)
            put(xh, xl, here, after, side)
            put(xh, xl, after, here, turn)

    def finish(s, cols):
        x, xh, xl, sh, sl = block(s)
        thin = product((xh[FIRST, :], xl[FIRST, :]), (xh[...], xl[...]))
        return 1.5 * x[FIRST, cols] - 0.5 * product(halves(thin), (xh[:, cols], xl[:, cols]))

    t1a_t, t2b_t = ham[a, 1].T, ham[b, 2].T
    turned[0] = t1a_t
    turned[1] = t2b_t
    d_a, d_b = on_a - level, on_b - level
    assemble(0, ((d_a, ham[a, 1], ham[a, 2]), (t1a_t, None, None), (ham[b, 1], None, d_b)))
    assemble(1, ((d_b, ham[b, 1], ham[b, 2]), (ham[a, 2], d_a, None), (t2b_t, None, None)))
    square(0, True, 1)
    square(1, True, 2)
    most_a = jnp.maximum(sums(d_a, t1a_t, ham[b, 1]), sums(ham[a, 2], d_b))
    most_b = jnp.maximum(sums(d_b, ham[a, 2], t2b_t), sums(ham[b, 1], d_a))
    part_a, part_b = sums(ham[a, 1]), sums(ham[b, 2])

    wait_all(got_note, recv.at[0])
    wait_all(got_packed, recv.at[1])

    below = (
        lax.broadcasted_iota(jnp.int32, (STRIP, BLK), 1)
        < lax.broadcasted_iota(jnp.int32, (STRIP, BLK), 0) + STRIP * n
    )

    def field(slot, i, rows):
        told = got_note[slot, :, BLK : 2 * BLK]
        return jnp.broadcast_to(told[:, FIELD * i : FIELD * i + 1], (rows, BLK))

    def offsets(j):
        slot = (PEERS - j) & (PEERS - 1)
        return field(slot, 0, STRIP), field(slot, 1, STRIP)

    def select(j, wanted, slots):
        chosen = slots(0)
        for k in range(1, PEERS):
            chosen = jnp.where(wanted == ((-j - k) & (PEERS - 1)), slots(k), chosen)
        return chosen

    def route_near(j):
        to_prev, to_next = offsets(j)
        return select(j, jnp.where(below, to_prev, to_next), lambda k: got_packed[k])

    for j in ORDER_OUT:
        pick_near[j] = route_near(j)
        push(pick_near.at[j], near.at[n], 4, j).start()
    near[n] = route_near(0)

    wait_all(got_next, recv.at[2])

    def route_far(j, ref):
        to_prev, to_next = offsets(j)
        ref[0:STRIP] = select(j, jnp.where(below, to_next, to_prev), lambda k: got_packed[k])
        ref[STRIP : 2 * STRIP] = select(j, to_prev, lambda k: got_next[k])

    for j in ORDER_OUT:
        route_far(j, pick_far.at[j])
        push(pick_far.at[j], far.at[n], 5, j).start()
    route_far(0, far.at[n])

    wait_all(got_prev, recv.at[3])

    def route_last(j):
        return select(j, offsets(j)[1], lambda k: got_prev[k])

    for j in ORDER_OUT:
        pick_last[j] = route_last(j)
        push(pick_last.at[j], last.at[n], 6, j).start()
    last[n] = route_last(0)

    to_prev, to_next = field(0, 0, 1), field(0, 1, 1)
    diag_prev, diag_next = [select(0, to, lambda k: got_note[k, :, 0:BLK]) for to in (to_prev, to_next)]
    live_prev = select(0, to_prev, lambda k: field(k, 3, 1))
    live_next = select(0, to_next, lambda k: field(k, 2, 1))

    def unpack(tile, low_diag):
        mirror = tile.T
        high = jnp.where(col >= row, tile, mirror)
        low = jnp.where(diagonal, low_diag, jnp.where(col < row, tile, mirror))
        return high, low

    wait_all(near, recv.at[4])
    on_next, on_prev = unpack(near[...].reshape(BLK, BLK), diag_prev)
    d_prev, d_next = on_prev - level, on_next - level
    complete(0, 1, d_prev)
    complete(1, 2, d_next)
    advance(0, scale_of(jnp.maximum(most_a, part_a + sums(d_prev))))
    advance(1, scale_of(jnp.maximum(most_b, part_b + sums(d_next))))
    for sweep in range(ITERS - 2):
        square(0)
        square(1)
        advance(0)
        advance(1)

    new_a = finish(0, ALL)
    new_b = finish(1, ALL)

    unit = jnp.where(diagonal, 1.0, 0.0)

    def fresh(new, index, j):
        x = new[:, tile(j)]
        value = 0.5 * (unit - x) if j == 0 else -0.5 * x
        return jnp.where(live[index] == 1, value, old[index, j].T)

    f0a, f1a, f2a = [fresh(new_a, a, j) for j in range(3)]
    f0b, f1b, f2b = [fresh(new_b, b, j) for j in range(3)]

    def emit(j, of_a, of_b):
        out[0, j] = jnp.where(forward, of_a, of_b)
        out[1, j] = jnp.where(forward, of_b, of_a)

    emit(0, 0.5 * (f0a + f0a.T), 0.5 * (f0b + f0b.T))
    inner = 0.5 * (f2a.T + f1b)
    out[0, 1] = f1a.T
    out[1, 1] = inner.T
    out[0, 2] = inner
    out[1, 2] = f2b.T

    wait_all(far, recv.at[5])
    wait_all(last, recv.at[6])
    on_prev_prev, on_next_next = unpack(far[:, 0:STRIP].reshape(BLK, BLK), diag_next)
    far_prev = far[:, STRIP : 2 * STRIP].reshape(BLK, BLK)
    far_prev_t = far_prev.T
    d_prev_prev = on_prev_prev - level
    on_next, on_prev = unpack(near[...].reshape(BLK, BLK), diag_prev)
    d_prev, d_next, d_a, d_b = on_prev - level, on_next - level, on_a - level, on_b - level
    assemble(2, ((d_prev, far_prev, turned[0]), (far_prev_t, d_prev_prev, None), (ham[a, 1], None, d_a)))
    scale_prev = scale_of(jnp.maximum(
        jnp.maximum(sums(d_prev, far_prev_t, ham[a, 1]), sums(far_prev, d_prev_prev)), sums(turned[0], d_a)
    ))
    far_next = last[...].reshape(BLK, BLK)
    far_next_t = far_next.T
    d_next_next = on_next_next - level
    assemble(3, ((d_next, turned[1], far_next), (ham[b, 2], d_b, None), (far_next_t, None, d_next_next)))
    scale_next = scale_of(jnp.maximum(
        jnp.maximum(sums(d_next, ham[b, 2], far_next_t), sums(turned[1], d_b)), sums(far_next, d_next_next)
    ))
    square(2, True)
    square(3, True)
    advance(2, scale_prev)
    advance(3, scale_next)
    for sweep in range(ITERS - 2):
        square(2)
        square(3)
        advance(2)
        advance(3)
    edge_prev = jnp.where(live_prev == 1.0, -0.5 * finish(2, tile(2)), far[:, STRIP : 2 * STRIP].reshape(BLK, BLK).T)
    edge_next = jnp.where(live_next == 1.0, -0.5 * finish(3, tile(1)), last[...].reshape(BLK, BLK).T)
    outer_a = 0.5 * (out[0, 1] + edge_prev)
    outer_b = 0.5 * (out[1, 2] + edge_next)
    emit(1, outer_a, out[1, 1])
    emit(2, out[0, 2], outer_b)

    for i, ref in enumerate((got_note, got_packed, got_next, got_prev, near, far, last)):
        wait_all(ref, send.at[i])


def shards(hamiltonian, old_density, neighbours, live, potential):
    hbm = pl.BlockSpec(memory_space=pltpu.HBM)
    strips = pltpu.VMEM((PEERS, STRIP, BLK), F32)
    two_strips = pltpu.VMEM((PEERS, 2 * STRIP, BLK), F32)
    matrices = pltpu.VMEM((4, ORDER, ORDER), F32)
    matrix_halves = pltpu.VMEM((4, ORDER, ORDER), BF16)
    return pl.pallas_call(
        kernel,
        out_shape=jax.ShapeDtypeStruct((2, 3, BLK, BLK), F32),
        in_specs=[hbm] * 5,
        out_specs=pl.BlockSpec(memory_space=pltpu.VMEM),
        scratch_shapes=[
            pltpu.VMEM((2, 3, BLK, BLK), F32),
            pltpu.VMEM((2, 3, BLK, BLK), F32),
            pltpu.SMEM((2, 3), jnp.int32),
            pltpu.SMEM((2,), jnp.int32),
            pltpu.SMEM((1,), F32),
            strips, strips, strips, pltpu.VMEM((1, 1, 2 * BLK), F32),
            strips, strips, strips, pltpu.VMEM((PEERS, 1, 2 * BLK), F32),
            strips, two_strips, strips, strips, two_strips, strips,
            pltpu.VMEM((2, BLK, BLK), F32),
            pltpu.VMEM((2, 2, BLK, BLK), F32),
            matrices, matrix_halves, matrix_halves, matrix_halves, matrix_halves,
            pltpu.SemaphoreType.DMA((5,)),
            pltpu.SemaphoreType.DMA((7,)),
            pltpu.SemaphoreType.DMA((7,)),
        ],
        compiler_params=pltpu.CompilerParams(
            collective_id=0, has_side_effects=True, vmem_limit_bytes=VMEM_LIMIT
        ),
        name="density",
    )(hamiltonian, old_density, neighbours, live, potential)


def solution(mesh):
    placed = (
        P(("wide", "narrow"), None, None, None),
        P(("wide", "narrow"), None, None, None),
        P(("wide", "narrow"), None),
        P(("wide", "narrow")),
        P(),
    )
    return jax.shard_map(
        shards,
        mesh=mesh,
        in_specs=placed,
        out_specs=P(("wide", "narrow"), None, None, None),
        check_vma=False,
    )
```

```python
import functools

import jax
import jax.numpy as jnp
from jax import lax
from jax.experimental import pallas as pl
from jax.experimental.pallas import tpu as pltpu
from jax.sharding import PartitionSpec as P

ITERS = 4
EPSILON = 1e-06
VMEM_LIMIT = 54_580 * 1024
BLK = 128
ORDER = 3 * BLK
PEERS = 16
STRIP = BLK // PEERS
FIELD = BLK // 4
ORDER_OUT = sorted(range(1, PEERS), key=lambda j: abs(j - PEERS // 2))
F32 = jnp.float32
BF16 = jnp.bfloat16
ALL, FIRST = slice(0, ORDER), slice(0, BLK)


def halves(x):
    high = x.astype(BF16)
    return high, (x - high.astype(F32)).astype(BF16)


def product(left, right):
    lh, ll = left
    rh, rl = right
    return jnp.dot(
        jnp.concatenate([lh, ll, lh], axis=1),
        jnp.concatenate([rh, rh, rl], axis=0),
        preferred_element_type=F32,
    )


def kernel(
    ham_hbm, old_hbm, nbr_hbm, live_hbm, pot_hbm, out,
    ham, old, nbr, live, pot,
    packed, outer_next, outer_prev, note, got_packed, got_next, got_prev, got_note,
    pick_near, pick_far, pick_last, near, far, last, turned, base,
    x_all, xh_all, xl_all, sh_all, sl_all,
    load, send, recv,
):
    w = lax.axis_index("wide")
    n = lax.axis_index("narrow")

    def peer(j):
        return (w, (n + j) & (PEERS - 1))

    inputs = ((nbr_hbm, nbr), (ham_hbm, ham), (live_hbm, live), (old_hbm, old), (pot_hbm, pot))
    loads = [pltpu.make_async_copy(src, dst, load.at[i]) for i, (src, dst) in enumerate(inputs)]
    for copy in loads:
        copy.start()

    barrier = pltpu.get_barrier_semaphore()

    def greet(j, _):
        pl.semaphore_signal(barrier, inc=1, device_id=peer(j), device_id_type=pl.DeviceIdType.MESH)
        return _

    lax.fori_loop(1, PEERS, greet, 0)

    for copy in loads:
        copy.wait()

    forward = nbr[0, 2] == 2 * n + 1
    a = jnp.where(forward, 0, 1)
    b = 1 - a
    live_a, live_b = live[a], live[b]

    row = lax.broadcasted_iota(jnp.int32, (BLK, BLK), 0)
    col = lax.broadcasted_iota(jnp.int32, (BLK, BLK), 1)
    diagonal = row == col
    on_a = ham[a, 0]
    on_b = ham[b, 0]
    packed[...] = jnp.where(col >= row, on_a, on_b).reshape(PEERS, STRIP, BLK)
    outer_prev[...] = jnp.where(live_a == 1, ham[a, 2], old[a, 1]).reshape(PEERS, STRIP, BLK)
    outer_next[...] = jnp.where(live_b == 1, ham[b, 1], old[b, 2]).reshape(PEERS, STRIP, BLK)
    note[0, :, 0:BLK] = jnp.sum(jnp.where(diagonal, on_b, 0.0), axis=0, keepdims=True)
    facts = (
        ((nbr[a, 1] >> 1) - n) & (PEERS - 1), ((nbr[b, 2] >> 1) - n) & (PEERS - 1), live_a, live_b,
    )
    lane = lax.broadcasted_iota(jnp.int32, (1, BLK), 1)
    told = jnp.full((1, BLK), facts[0], jnp.int32)
    for i in range(1, 4):
        told = jnp.where(lane >= FIELD * i, facts[i], told)
    note[0, :, BLK : 2 * BLK] = told.astype(F32)

    def push(src, dst, which, j):
        return pltpu.make_async_remote_copy(
            src_ref=src, dst_ref=dst, send_sem=send.at[which], recv_sem=recv.at[which],
            device_id=peer(j), device_id_type=pl.DeviceIdType.MESH,
        )

    def wait_all(ref, sem):
        many = ref.at[pl.ds(1, PEERS - 1)]
        pltpu.make_async_copy(many, many, sem).wait()

    pl.semaphore_wait(barrier, PEERS - 1)

    def to_all(*moves):
        def step(m, _):
            j = PEERS // 2 + (1 - 2 * (m & 1)) * ((m + 1) >> 1)
            for src, dst, which in moves:
                push(src.at[0 if src is note else (n + j) & (PEERS - 1)], dst.at[j], which, j).start()
            return _

        lax.fori_loop(0, PEERS - 1, step, 0)

    to_all((note, got_note, 0), (packed, got_packed, 1))
    to_all((outer_next, got_next, 2))
    to_all((outer_prev, got_prev, 3))
    got_note[0] = note[0]
    got_packed[0] = packed[n]
    got_next[0] = outer_next[n]
    got_prev[0] = outer_prev[n]

    level = jnp.where(diagonal, pot[0], 0.0)

    def block(s):
        return x_all.at[s], xh_all.at[s], xl_all.at[s], sh_all.at[s], sl_all.at[s]

    def tile(i):
        return slice(BLK * i, BLK * i + BLK)

    def put(high, low, rows, cols, value):
        high[rows, cols], low[rows, cols] = halves(value)

    def sums(*tiles):
        return functools.reduce(jnp.add, [jnp.sum(jnp.abs(t), axis=0, keepdims=True) for t in tiles])

    def scale_of(most):
        return 1.0 / (jnp.max(most, axis=1, keepdims=True) + EPSILON)

    def assemble(s, tiles):
        x, xh, xl, sh, sl = block(s)
        for i in range(3):
            for k in range(3):
                if tiles[i][k] is not None:
                    x[tile(i), tile(k)] = tiles[i][k]
                    put(xh, xl, tile(i), tile(k), tiles[i][k])

    def symmetric(left, right, first):
        def strip(ref, i, inner):
            return jnp.concatenate([ref[tile(i), tile(k)] for k in inner], axis=1)

        def pair(ref, i, inner):
            return jnp.concatenate([
                jnp.concatenate([ref[tile(k), tile(i)], ref[tile(k), tile((i + 1) % 3)]], axis=1)
                for k in inner
            ], axis=0)

        results = []
        for i in range(3):
            inner = (0, i) if first and i > 0 else (0, 1, 2)
            results.append(product(
                tuple(strip(ref, i, inner) for ref in left), tuple(pair(ref, i, inner) for ref in right)
            ))
        return results

    def square(s, first=False, keep=None):
        x, xh, xl, sh, sl = block(s)
        for i, both in enumerate(symmetric((xh, xl), (xh, xl), first)):
            here, after = tile(i), tile((i + 1) % 3)
            own, side = both[:, 0:BLK], both[:, BLK : 2 * BLK]
            if not first:
                own, side = jnp.where(diagonal, 1.5, 0.0) - 0.5 * own, -0.5 * side
            put(sh, sl, here, here, own)
            put(sh, sl, here, after, side)
            put(sh, sl, after, here, side.T)
            if keep is not None and i == keep:
                base[s, 0] = own
            if keep is not None and i == 0 and keep == 1:
                base[s, 1] = side.T
            if keep is not None and i == 2 and keep == 2:
                base[s, 1] = side

    def complete(s, u, value):
        x, xh, xl, sh, sl = block(s)
        mine = tile(u)
        x[mine, mine] = value
        vh, vl = halves(value)
        xh[mine, mine], xl[mine, mine] = vh, vl
        more = product(
            (vh, vl),
            (
                jnp.concatenate([xh[mine, FIRST], vh], axis=1),
                jnp.concatenate([xl[mine, FIRST], vl], axis=1),
            ),
        )
        side = base[s, 1] + more[:, 0:BLK]
        put(sh, sl, mine, FIRST, side)
        put(sh, sl, FIRST, mine, side.T)
        put(sh, sl, mine, mine, base[s, 0] + more[:, BLK : 2 * BLK])

    def advance(s, scale=None, final=False):
        x, xh, xl, sh, sl = block(s)
        for i, both in enumerate(symmetric((xh, xl), (sh, sl), scale is not None)):
            here, after = tile(i), tile((i + 1) % 3)
            own, side = both[:, 0:BLK], both[:, BLK : 2 * BLK]
            if scale is not None:
                once, thrice = 1.5 * scale, 0.5 * scale * scale * scale
                own = once * x[here, here] - thrice * own
                side = once * x[here, after] - thrice * side
            turn = side.T
            if final and i == 0:
                x[here, here] = own
                x[here, after] = side
            if final and i == 2:
                x[after, here] = turn
            put(xh, xl, here, here, own)
            put(xh, xl, here, after, side)
            put(xh, xl, after, here, turn)

    def finish(s, cols):
        x, xh, xl, sh, sl = block(s)
        thin = product((xh[FIRST, :], xl[FIRST, :]), (xh[...], xl[...]))
        return 1.5 * x[FIRST, cols] - 0.5 * product(halves(thin), (xh[:, cols], xl[:, cols]))

    t1a_t, t2b_t = ham[a, 1].T, ham[b, 2].T
    turned[0] = t1a_t
    turned[1] = t2b_t
    d_a, d_b = on_a - level, on_b - level
    none, nil = (None, None, None), jnp.zeros((BLK, BLK), F32)
    assemble(0, ((d_a, ham[a, 1], ham[a, 2]), (t1a_t, nil, nil), (ham[b, 1], nil, d_b)))
    assemble(1, ((d_b, ham[b, 1], ham[b, 2]), (ham[a, 2], d_a, nil), (t2b_t, nil, nil)))
    assemble(2, ((None, None, t1a_t), (None, None, nil), (ham[a, 1], nil, d_a)))
    assemble(3, ((None, t2b_t, None), (ham[b, 2], d_b, nil), (None, nil, None)))
    square(0, True, 1)
    square(1, True, 2)
    most_a = jnp.maximum(sums(d_a, t1a_t, ham[b, 1]), sums(ham[a, 2], d_b))
    most_b = jnp.maximum(sums(d_b, ham[a, 2], t2b_t), sums(ham[b, 1], d_a))
    most_prev, most_next = sums(t1a_t, d_a), sums(t2b_t, d_b)
    part_a, part_b = sums(ham[a, 1]), sums(ham[b, 2])

    wait_all(got_note, recv.at[0])
    wait_all(got_packed, recv.at[1])

    below = (
        lax.broadcasted_iota(jnp.int32, (STRIP, BLK), 1)
        < lax.broadcasted_iota(jnp.int32, (STRIP, BLK), 0) + STRIP * n
    )

    def field(slot, i, rows):
        told = got_note[slot, :, BLK : 2 * BLK]
        return jnp.broadcast_to(told[:, FIELD * i : FIELD * i + 1], (rows, BLK))

    def offsets(j):
        slot = (PEERS - j) & (PEERS - 1)
        return field(slot, 0, STRIP), field(slot, 1, STRIP)

    def select(j, wanted, slots):
        chosen = slots(0)
        for k in range(1, PEERS):
            chosen = jnp.where(wanted == ((-j - k) & (PEERS - 1)), slots(k), chosen)
        return chosen

    def route_near(j):
        to_prev, to_next = offsets(j)
        return select(j, jnp.where(below, to_prev, to_next), lambda k: got_packed[k])

    for j in ORDER_OUT:
        pick_near[j] = route_near(j)
        push(pick_near.at[j], near.at[n], 4, j).start()
    near[n] = route_near(0)

    wait_all(got_next, recv.at[2])

    def route_far(j, ref):
        to_prev, to_next = offsets(j)
        ref[0:STRIP] = select(j, jnp.where(below, to_next, to_prev), lambda k: got_packed[k])
        ref[STRIP : 2 * STRIP] = select(j, to_prev, lambda k: got_next[k])

    for j in ORDER_OUT:
        route_far(j, pick_far.at[j])
        push(pick_far.at[j], far.at[n], 5, j).start()
    route_far(0, far.at[n])

    wait_all(got_prev, recv.at[3])

    def route_last(j):
        return select(j, offsets(j)[1], lambda k: got_prev[k])

    for j in ORDER_OUT:
        pick_last[j] = route_last(j)
        push(pick_last.at[j], last.at[n], 6, j).start()
    last[n] = route_last(0)

    to_prev, to_next = field(0, 0, 1), field(0, 1, 1)
    diag_prev, diag_next = [select(0, to, lambda k: got_note[k, :, 0:BLK]) for to in (to_prev, to_next)]
    live_prev = select(0, to_prev, lambda k: field(k, 3, 1))
    live_next = select(0, to_next, lambda k: field(k, 2, 1))

    def unpack(tile, low_diag):
        mirror = tile.T
        high = jnp.where(col >= row, tile, mirror)
        low = jnp.where(diagonal, low_diag, jnp.where(col < row, tile, mirror))
        return high, low

    wait_all(near, recv.at[4])
    on_next, on_prev = unpack(near[...].reshape(BLK, BLK), diag_prev)
    d_prev, d_next = on_prev - level, on_next - level
    complete(0, 1, d_prev)
    complete(1, 2, d_next)
    assemble(2, ((d_prev, None, None), none, none))
    assemble(3, ((d_next, None, None), none, none))
    part_prev, part_next = part_a + sums(d_prev), part_b + sums(d_next)
    advance(0, scale_of(jnp.maximum(most_a, part_a + sums(d_prev))))
    advance(1, scale_of(jnp.maximum(most_b, part_b + sums(d_next))))
    for sweep in range(ITERS - 2):
        square(0)
        square(1)
        advance(0, final=sweep == ITERS - 3)
        advance(1, final=sweep == ITERS - 3)

    new_a = finish(0, ALL)
    new_b = finish(1, ALL)

    unit = jnp.where(diagonal, 1.0, 0.0)

    def fresh(new, index, j):
        x = new[:, tile(j)]
        value = 0.5 * (unit - x) if j == 0 else -0.5 * x
        return jnp.where(live[index] == 1, value, old[index, j].T)

    f0a, f1a, f2a = [fresh(new_a, a, j) for j in range(3)]
    f0b, f1b, f2b = [fresh(new_b, b, j) for j in range(3)]

    def emit(j, of_a, of_b):
        out[0, j] = jnp.where(forward, of_a, of_b)
        out[1, j] = jnp.where(forward, of_b, of_a)

    emit(0, 0.5 * (f0a + f0a.T), 0.5 * (f0b + f0b.T))
    inner = 0.5 * (f2a.T + f1b)
    out[0, 1] = f1a.T
    out[1, 1] = inner.T
    out[0, 2] = inner
    out[1, 2] = f2b.T

    wait_all(far, recv.at[5])
    on_prev_prev, on_next_next = unpack(far[:, 0:STRIP].reshape(BLK, BLK), diag_next)
    far_prev = far[:, STRIP : 2 * STRIP].reshape(BLK, BLK)
    far_prev_t = far_prev.T
    d_prev_prev, d_next_next = on_prev_prev - level, on_next_next - level
    assemble(2, ((None, far_prev, None), (far_prev_t, d_prev_prev, None), none))
    assemble(3, (none, none, (None, None, d_next_next)))
    square(2, True)
    base[0, 0] = far_prev_t
    scale_prev = scale_of(jnp.maximum(
        jnp.maximum(part_prev + sums(far_prev_t), most_prev), sums(far_prev, d_prev_prev)
    ))
    last_sums = sums(d_next_next)
    wait_all(last, recv.at[6])
    far_next = last[...].reshape(BLK, BLK)
    far_next_t = far_next.T
    assemble(3, ((None, None, far_next), none, (far_next_t, None, None)))
    square(3, True)
    base[0, 1] = far_next_t
    scale_next = scale_of(jnp.maximum(
        jnp.maximum(part_next + sums(far_next_t), most_next), sums(far_next) + last_sums
    ))
    advance(2, scale_prev)
    advance(3, scale_next)
    for sweep in range(ITERS - 2):
        square(2)
        square(3)
        advance(2, final=sweep == ITERS - 3)
        advance(3, final=sweep == ITERS - 3)
    edge_prev = jnp.where(live_prev == 1.0, -0.5 * finish(2, tile(2)), base[0, 0])
    edge_next = jnp.where(live_next == 1.0, -0.5 * finish(3, tile(1)), base[0, 1])
    outer_a = 0.5 * (out[0, 1] + edge_prev)
    outer_b = 0.5 * (out[1, 2] + edge_next)
    emit(1, outer_a, out[1, 1])
    emit(2, out[0, 2], outer_b)

    for i, ref in enumerate((got_note, got_packed, got_next, got_prev, near, far, last)):
        wait_all(ref, send.at[i])


def shards(hamiltonian, old_density, neighbours, live, potential):
    hbm = pl.BlockSpec(memory_space=pltpu.HBM)
    strips = pltpu.VMEM((PEERS, STRIP, BLK), F32)
    two_strips = pltpu.VMEM((PEERS, 2 * STRIP, BLK), F32)
    matrices = pltpu.VMEM((4, ORDER, ORDER), F32)
    matrix_halves = pltpu.VMEM((4, ORDER, ORDER), BF16)
    return pl.pallas_call(
        kernel,
        out_shape=jax.ShapeDtypeStruct((2, 3, BLK, BLK), F32),
        in_specs=[hbm] * 5,
        out_specs=pl.BlockSpec(memory_space=pltpu.VMEM),
        scratch_shapes=[
            pltpu.VMEM((2, 3, BLK, BLK), F32),
            pltpu.VMEM((2, 3, BLK, BLK), F32),
            pltpu.SMEM((2, 3), jnp.int32),
            pltpu.SMEM((2,), jnp.int32),
            pltpu.SMEM((1,), F32),
            strips, strips, strips, pltpu.VMEM((1, 1, 2 * BLK), F32),
            strips, strips, strips, pltpu.VMEM((PEERS, 1, 2 * BLK), F32),
            strips, two_strips, strips, strips, two_strips, strips,
            pltpu.VMEM((2, BLK, BLK), F32),
            pltpu.VMEM((2, 2, BLK, BLK), F32),
            matrices, matrix_halves, matrix_halves, matrix_halves, matrix_halves,
            pltpu.SemaphoreType.DMA((5,)),
            pltpu.SemaphoreType.DMA((7,)),
            pltpu.SemaphoreType.DMA((7,)),
        ],
        compiler_params=pltpu.CompilerParams(
            collective_id=0, has_side_effects=True, vmem_limit_bytes=VMEM_LIMIT
        ),
        name="density",
    )(hamiltonian, old_density, neighbours, live, potential)


def solution(mesh):
    placed = (
        P(("wide", "narrow"), None, None, None),
        P(("wide", "narrow"), None, None, None),
        P(("wide", "narrow"), None),
        P(("wide", "narrow")),
        P(),
    )
    return jax.shard_map(
        shards,
        mesh=mesh,
        in_specs=placed,
        out_specs=P(("wide", "narrow"), None, None, None),
        check_vma=False,
    )
```

```python
import functools

import jax
import jax.numpy as jnp
from jax import lax
from jax.experimental import pallas as pl
from jax.experimental.pallas import tpu as pltpu
from jax.sharding import PartitionSpec as P

ITERS = 4
EPSILON = 1e-06
VMEM_LIMIT = 54_580 * 1024
BLK = 128
ORDER = 3 * BLK
PEERS = 16
STRIP = BLK // PEERS
FIELD = BLK // 4
ORDER_OUT = sorted(range(1, PEERS), key=lambda j: abs(j - PEERS // 2))
F32 = jnp.float32
BF16 = jnp.bfloat16
ALL, FIRST = slice(0, ORDER), slice(0, BLK)


def halves(x):
    high = x.astype(BF16)
    return high, (x - high.astype(F32)).astype(BF16)


def product(left, right):
    lh, ll = left
    rh, rl = right
    return jnp.dot(
        jnp.concatenate([lh, ll, lh], axis=1),
        jnp.concatenate([rh, rh, rl], axis=0),
        preferred_element_type=F32,
    )


def kernel(
    ham_hbm, old_hbm, nbr_hbm, live_hbm, pot_hbm, out,
    ham, old, nbr, live, pot,
    packed, outer_next, outer_prev, note, got_packed, got_next, got_prev, got_note,
    pick_near, pick_onsite, pick_far, pick_last, near, onsite, far, last, turned, base,
    x_all, xh_all, xl_all, sh_all, sl_all,
    load, send, recv,
):
    w = lax.axis_index("wide")
    n = lax.axis_index("narrow")

    def peer(j):
        return (w, (n + j) & (PEERS - 1))

    barrier = pltpu.get_barrier_semaphore()

    def far_first(m):
        return PEERS // 2 + (1 - 2 * (m & 1)) * ((m + 1) >> 1)

    def greet(m, _):
        j = far_first(m)
        pl.semaphore_signal(barrier, inc=1, device_id=peer(j), device_id_type=pl.DeviceIdType.MESH)
        return _

    lax.fori_loop(0, PEERS - 1, greet, 0)

    inputs = ((nbr_hbm, nbr), (ham_hbm, ham), (live_hbm, live), (old_hbm, old), (pot_hbm, pot))
    loads = [pltpu.make_async_copy(src, dst, load.at[i]) for i, (src, dst) in enumerate(inputs)]
    for copy in loads:
        copy.start()

    for copy in loads:
        copy.wait()

    forward = nbr[0, 2] == 2 * n + 1
    a = jnp.where(forward, 0, 1)
    b = 1 - a
    live_a, live_b = live[a], live[b]

    row = lax.broadcasted_iota(jnp.int32, (BLK, BLK), 0)
    col = lax.broadcasted_iota(jnp.int32, (BLK, BLK), 1)
    diagonal = row == col
    on_a = ham[a, 0]
    on_b = ham[b, 0]
    packed[...] = jnp.where(col >= row, on_a, on_b).reshape(PEERS, STRIP, BLK)
    outer_prev[...] = jnp.where(live_a == 1, ham[a, 2], old[a, 1]).reshape(PEERS, STRIP, BLK)
    outer_next[...] = jnp.where(live_b == 1, ham[b, 1], old[b, 2]).reshape(PEERS, STRIP, BLK)
    note[0, :, 0:BLK] = jnp.sum(jnp.where(diagonal, on_b, 0.0), axis=0, keepdims=True)
    facts = (
        ((nbr[a, 1] >> 1) - n) & (PEERS - 1), ((nbr[b, 2] >> 1) - n) & (PEERS - 1), live_a, live_b,
    )
    lane = lax.broadcasted_iota(jnp.int32, (1, BLK), 1)
    told = jnp.full((1, BLK), facts[0], jnp.int32)
    for i in range(1, 4):
        told = jnp.where(lane >= FIELD * i, facts[i], told)
    note[0, :, BLK : 2 * BLK] = told.astype(F32)

    def push(src, dst, which, j):
        return pltpu.make_async_remote_copy(
            src_ref=src, dst_ref=dst, send_sem=send.at[which], recv_sem=recv.at[which],
            device_id=peer(j), device_id_type=pl.DeviceIdType.MESH,
        )

    def wait_all(ref, sem):
        many = ref.at[pl.ds(1, PEERS - 1)]
        pltpu.make_async_copy(many, many, sem).wait()

    pl.semaphore_wait(barrier, PEERS - 1)

    def to_all(*moves):
        def step(m, _):
            j = far_first(m)
            for src, dst, which in moves:
                push(src.at[0 if src is note else (n + j) & (PEERS - 1)], dst.at[j], which, j).start()
            return _

        lax.fori_loop(0, PEERS - 1, step, 0)

    to_all((note, got_note, 0), (packed, got_packed, 1))
    to_all((outer_next, got_next, 2))
    to_all((outer_prev, got_prev, 3))
    got_note[0] = note[0]
    got_packed[0] = packed[n]
    got_next[0] = outer_next[n]
    got_prev[0] = outer_prev[n]

    level = jnp.where(diagonal, pot[0], 0.0)

    def block(s):
        return x_all.at[s], xh_all.at[s], xl_all.at[s], sh_all.at[s], sl_all.at[s]

    def tile(i):
        return slice(BLK * i, BLK * i + BLK)

    def put(high, low, rows, cols, value):
        high[rows, cols], low[rows, cols] = halves(value)

    def sums(*tiles):
        return functools.reduce(jnp.add, [jnp.sum(jnp.abs(t), axis=0, keepdims=True) for t in tiles])

    def scale_of(most):
        return 1.0 / (jnp.max(most, axis=1, keepdims=True) + EPSILON)

    def assemble(s, tiles):
        x, xh, xl, sh, sl = block(s)
        for i in range(3):
            for k in range(3):
                if tiles[i][k] is not None:
                    x[tile(i), tile(k)] = tiles[i][k]
                    put(xh, xl, tile(i), tile(k), tiles[i][k])

    def symmetric(left, right, first):
        def strip(ref, i, inner):
            return jnp.concatenate([ref[tile(i), tile(k)] for k in inner], axis=1)

        def pair(ref, i, inner):
            return jnp.concatenate([
                jnp.concatenate([ref[tile(k), tile(i)], ref[tile(k), tile((i + 1) % 3)]], axis=1)
                for k in inner
            ], axis=0)

        results = []
        for i in range(3):
            inner = (0, i) if first and i > 0 else (0, 1, 2)
            results.append(product(
                tuple(strip(ref, i, inner) for ref in left), tuple(pair(ref, i, inner) for ref in right)
            ))
        return results

    def square(s, first=False, keep=None):
        x, xh, xl, sh, sl = block(s)
        for i, both in enumerate(symmetric((xh, xl), (xh, xl), first)):
            here, after = tile(i), tile((i + 1) % 3)
            own, side = both[:, 0:BLK], both[:, BLK : 2 * BLK]
            if not first:
                own, side = jnp.where(diagonal, 1.5, 0.0) - 0.5 * own, -0.5 * side
            put(sh, sl, here, here, own)
            put(sh, sl, here, after, side)
            put(sh, sl, after, here, side.T)
            if keep is not None and i == keep:
                base[s, 0] = own
            if keep is not None and i == 0 and keep == 1:
                base[s, 1] = side.T
            if keep is not None and i == 2 and keep == 2:
                base[s, 1] = side

    def complete(s, u, value):
        x, xh, xl, sh, sl = block(s)
        mine = tile(u)
        x[mine, mine] = value
        vh, vl = halves(value)
        xh[mine, mine], xl[mine, mine] = vh, vl
        more = product(
            (vh, vl),
            (
                jnp.concatenate([xh[mine, FIRST], vh], axis=1),
                jnp.concatenate([xl[mine, FIRST], vl], axis=1),
            ),
        )
        side = base[s, 1] + more[:, 0:BLK]
        put(sh, sl, mine, FIRST, side)
        put(sh, sl, FIRST, mine, side.T)
        put(sh, sl, mine, mine, base[s, 0] + more[:, BLK : 2 * BLK])

    def advance(s, scale=None, final=False):
        x, xh, xl, sh, sl = block(s)
        for i, both in enumerate(symmetric((xh, xl), (sh, sl), scale is not None)):
            here, after = tile(i), tile((i + 1) % 3)
            own, side = both[:, 0:BLK], both[:, BLK : 2 * BLK]
            if scale is not None:
                once, thrice = 1.5 * scale, 0.5 * scale * scale * scale
                own = once * x[here, here] - thrice * own
                side = once * x[here, after] - thrice * side
            turn = side.T
            if final and i == 0:
                x[here, here] = own
                x[here, after] = side
            if final and i == 2:
                x[after, here] = turn
            put(xh, xl, here, here, own)
            put(xh, xl, here, after, side)
            put(xh, xl, after, here, turn)

    def finish(s, cols):
        x, xh, xl, sh, sl = block(s)
        thin = product((xh[FIRST, :], xl[FIRST, :]), (xh[...], xl[...]))
        return 1.5 * x[FIRST, cols] - 0.5 * product(halves(thin), (xh[:, cols], xl[:, cols]))

    t1a_t, t2b_t = ham[a, 1].T, ham[b, 2].T
    turned[0] = t1a_t
    turned[1] = t2b_t
    d_a, d_b = on_a - level, on_b - level
    none, nil = (None, None, None), jnp.zeros((BLK, BLK), F32)
    assemble(0, ((d_a, ham[a, 1], ham[a, 2]), (t1a_t, nil, nil), (ham[b, 1], nil, d_b)))
    assemble(1, ((d_b, ham[b, 1], ham[b, 2]), (ham[a, 2], d_a, nil), (t2b_t, nil, nil)))
    assemble(2, ((None, None, t1a_t), (None, None, nil), (ham[a, 1], nil, d_a)))
    assemble(3, ((None, t2b_t, None), (ham[b, 2], d_b, nil), (None, nil, None)))
    square(0, True, 1)
    square(1, True, 2)
    most_a = jnp.maximum(sums(d_a, t1a_t, ham[b, 1]), sums(ham[a, 2], d_b))
    most_b = jnp.maximum(sums(d_b, ham[a, 2], t2b_t), sums(ham[b, 1], d_a))
    most_prev, most_next = sums(t1a_t, d_a), sums(t2b_t, d_b)
    part_a, part_b = sums(ham[a, 1]), sums(ham[b, 2])

    wait_all(got_note, recv.at[0])
    wait_all(got_packed, recv.at[1])

    below = (
        lax.broadcasted_iota(jnp.int32, (STRIP, BLK), 1)
        < lax.broadcasted_iota(jnp.int32, (STRIP, BLK), 0) + STRIP * n
    )

    def field(slot, i, rows):
        told = got_note[slot, :, BLK : 2 * BLK]
        return jnp.broadcast_to(told[:, FIELD * i : FIELD * i + 1], (rows, BLK))

    def offsets(j):
        slot = (PEERS - j) & (PEERS - 1)
        return field(slot, 0, STRIP), field(slot, 1, STRIP)

    def select(j, wanted, slots):
        chosen = slots(0)
        for k in range(1, PEERS):
            chosen = jnp.where(wanted == ((-j - k) & (PEERS - 1)), slots(k), chosen)
        return chosen

    def route_near(j):
        to_prev, to_next = offsets(j)
        return select(j, jnp.where(below, to_prev, to_next), lambda k: got_packed[k])

    for j in ORDER_OUT:
        pick_near[j] = route_near(j)
        push(pick_near.at[j], near.at[n], 4, j).start()
    near[n] = route_near(0)

    def route_onsite(j):
        to_prev, to_next = offsets(j)
        return select(j, jnp.where(below, to_next, to_prev), lambda k: got_packed[k])

    for j in ORDER_OUT:
        pick_onsite[j] = route_onsite(j)
        push(pick_onsite.at[j], onsite.at[n], 7, j).start()
    onsite[n] = route_onsite(0)

    wait_all(got_next, recv.at[2])

    def route_far(j):
        return select(j, offsets(j)[0], lambda k: got_next[k])

    for j in ORDER_OUT:
        pick_far[j] = route_far(j)
        push(pick_far.at[j], far.at[n], 5, j).start()
    far[n] = route_far(0)

    wait_all(got_prev, recv.at[3])

    def route_last(j):
        return select(j, offsets(j)[1], lambda k: got_prev[k])

    for j in ORDER_OUT:
        pick_last[j] = route_last(j)
        push(pick_last.at[j], last.at[n], 6, j).start()
    last[n] = route_last(0)

    to_prev, to_next = field(0, 0, 1), field(0, 1, 1)
    diag_prev, diag_next = [select(0, to, lambda k: got_note[k, :, 0:BLK]) for to in (to_prev, to_next)]
    live_prev = select(0, to_prev, lambda k: field(k, 3, 1))
    live_next = select(0, to_next, lambda k: field(k, 2, 1))

    def unpack(tile, low_diag):
        mirror = tile.T
        high = jnp.where(col >= row, tile, mirror)
        low = jnp.where(diagonal, low_diag, jnp.where(col < row, tile, mirror))
        return high, low

    wait_all(near, recv.at[4])
    on_next, on_prev = unpack(near[...].reshape(BLK, BLK), diag_prev)
    d_prev, d_next = on_prev - level, on_next - level
    complete(0, 1, d_prev)
    complete(1, 2, d_next)
    assemble(2, ((d_prev, None, None), none, none))
    assemble(3, ((d_next, None, None), none, none))
    part_prev, part_next = part_a + sums(d_prev), part_b + sums(d_next)
    advance(0, scale_of(jnp.maximum(most_a, part_a + sums(d_prev))))
    advance(1, scale_of(jnp.maximum(most_b, part_b + sums(d_next))))
    for sweep in range(ITERS - 2):
        square(0)
        square(1)
        advance(0, final=sweep == ITERS - 3)
        advance(1, final=sweep == ITERS - 3)

    new_a = finish(0, ALL)
    new_b = finish(1, ALL)

    unit = jnp.where(diagonal, 1.0, 0.0)

    def fresh(new, index, j):
        x = new[:, tile(j)]
        value = 0.5 * (unit - x) if j == 0 else -0.5 * x
        return jnp.where(live[index] == 1, value, old[index, j].T)

    f0a, f1a, f2a = [fresh(new_a, a, j) for j in range(3)]
    f0b, f1b, f2b = [fresh(new_b, b, j) for j in range(3)]

    def emit(j, of_a, of_b):
        out[0, j] = jnp.where(forward, of_a, of_b)
        out[1, j] = jnp.where(forward, of_b, of_a)

    emit(0, 0.5 * (f0a + f0a.T), 0.5 * (f0b + f0b.T))
    inner = 0.5 * (f2a.T + f1b)
    out[0, 1] = f1a.T
    out[1, 1] = inner.T
    out[0, 2] = inner
    out[1, 2] = f2b.T

    wait_all(onsite, recv.at[7])
    on_prev_prev, on_next_next = unpack(onsite[...].reshape(BLK, BLK), diag_next)
    d_prev_prev, d_next_next = on_prev_prev - level, on_next_next - level
    assemble(2, (none, (None, d_prev_prev, None), none))
    assemble(3, (none, none, (None, None, d_next_next)))
    first_sums, last_sums = sums(d_prev_prev), sums(d_next_next)

    wait_all(far, recv.at[5])
    far_prev = far[...].reshape(BLK, BLK)
    far_prev_t = far_prev.T
    assemble(2, ((None, far_prev, None), (far_prev_t, None, None), none))
    square(2, True)
    base[0, 0] = far_prev_t
    scale_prev = scale_of(jnp.maximum(
        jnp.maximum(part_prev + sums(far_prev_t), most_prev), sums(far_prev) + first_sums
    ))
    wait_all(last, recv.at[6])
    far_next = last[...].reshape(BLK, BLK)
    far_next_t = far_next.T
    assemble(3, ((None, None, far_next), none, (far_next_t, None, None)))
    square(3, True)
    base[0, 1] = far_next_t
    scale_next = scale_of(jnp.maximum(
        jnp.maximum(part_next + sums(far_next_t), most_next), sums(far_next) + last_sums
    ))
    advance(2, scale_prev)
    advance(3, scale_next)
    for sweep in range(ITERS - 2):
        square(2)
        square(3)
        advance(2, final=sweep == ITERS - 3)
        advance(3, final=sweep == ITERS - 3)
    edge_prev = jnp.where(live_prev == 1.0, -0.5 * finish(2, tile(2)), base[0, 0])
    edge_next = jnp.where(live_next == 1.0, -0.5 * finish(3, tile(1)), base[0, 1])
    outer_a = 0.5 * (out[0, 1] + edge_prev)
    outer_b = 0.5 * (out[1, 2] + edge_next)
    emit(1, outer_a, out[1, 1])
    emit(2, out[0, 2], outer_b)

    for i, ref in enumerate((got_note, got_packed, got_next, got_prev, near, far, last, onsite)):
        wait_all(ref, send.at[i])


def shards(hamiltonian, old_density, neighbours, live, potential):
    hbm = pl.BlockSpec(memory_space=pltpu.HBM)
    strips = pltpu.VMEM((PEERS, STRIP, BLK), F32)
    matrices = pltpu.VMEM((4, ORDER, ORDER), F32)
    matrix_halves = pltpu.VMEM((4, ORDER, ORDER), BF16)
    return pl.pallas_call(
        kernel,
        out_shape=jax.ShapeDtypeStruct((2, 3, BLK, BLK), F32),
        in_specs=[hbm] * 5,
        out_specs=pl.BlockSpec(memory_space=pltpu.VMEM),
        scratch_shapes=[
            pltpu.VMEM((2, 3, BLK, BLK), F32),
            pltpu.VMEM((2, 3, BLK, BLK), F32),
            pltpu.SMEM((2, 3), jnp.int32),
            pltpu.SMEM((2,), jnp.int32),
            pltpu.SMEM((1,), F32),
            strips, strips, strips, pltpu.VMEM((1, 1, 2 * BLK), F32),
            strips, strips, strips, pltpu.VMEM((PEERS, 1, 2 * BLK), F32),
            strips, strips, strips, strips, strips, strips, strips, strips,
            pltpu.VMEM((2, BLK, BLK), F32),
            pltpu.VMEM((2, 2, BLK, BLK), F32),
            matrices, matrix_halves, matrix_halves, matrix_halves, matrix_halves,
            pltpu.SemaphoreType.DMA((5,)),
            pltpu.SemaphoreType.DMA((8,)),
            pltpu.SemaphoreType.DMA((8,)),
        ],
        compiler_params=pltpu.CompilerParams(
            collective_id=0, has_side_effects=True, vmem_limit_bytes=VMEM_LIMIT
        ),
        name="density",
    )(hamiltonian, old_density, neighbours, live, potential)


def solution(mesh):
    placed = (
        P(("wide", "narrow"), None, None, None),
        P(("wide", "narrow"), None, None, None),
        P(("wide", "narrow"), None),
        P(("wide", "narrow")),
        P(),
    )
    return jax.shard_map(
        shards,
        mesh=mesh,
        in_specs=placed,
        out_specs=P(("wide", "narrow"), None, None, None),
        check_vma=False,
    )
```
